32 devices in a mesh: gx: 16 (over z, x, core), gy: 2 (over y).
Axes of the slice: x: 2, y: 2, z: 4, core: 2. Of those that a mesh axis runs over, the one named last changes fastest.
Arguments:
- tokens: bfloat16 [2304, 4608], P('gx', 'gy'), may hold values from -6 to 6
- pre_gain: bfloat16 [4608], P('gy'), may hold values from -0.5 to 0.5
- w_q: bfloat16 [4608, 4096], P('gx', 'gy'), may hold values from -0.09375 to 0.09375
- w_k: bfloat16 [4608, 2048], P('gx', 'gy'), may hold values from -0.09375 to 0.09375
- w_v: bfloat16 [4608, 2048], P('gx', 'gy'), may hold values from -0.09375 to 0.09375
- w_o: bfloat16 [4096, 4608], P('gy', 'gx')
- post_gain: bfloat16 [4608], P('gy'), may hold values from -0.5 to 0.5
- k_cache: bfloat16 [16384, 2048], P('gx', 'gy'), may hold values from -6 to 6
- v_cache: bfloat16 [16384, 2048], P('gx', 'gy')
- cached_len: int32 [12], replicated, may hold values from 1 to 5120, as said below
- new_len: int32 [12], replicated, may hold values from 48 to 192, as said below
- slot_offset: int32 [12], replicated, may hold values from 0 to 16191, as said below
Outputs:
- layer_out: bfloat16 [2304, 4608], P('gx', 'gy')
- k_pool: bfloat16 [16384, 2048], P('gx', 'gy')
- v_pool: bfloat16 [16384, 2048], P('gx', 'gy')
The draws below stay inside these ranges and needn't reach their ends.
Inputs may be any that keep to these rules, and one draw needn't show every extreme that they name: `cached_len`: two requests are long: one has exactly 5120 cached tokens, the other between 4929 and 5120; the others have at most 256, and one of them has exactly 1. `new_len`: some request has all 192 slots real. Request r owns pool slots slot_offset[r] to slot_offset[r] + cached_len[r] + 191; these regions are disjoint and lie inside the pool; one starts at slot 0 and one ends at the pool's last slot.
All inputs are finite; a program needn't handle non-finite values.
Results may differ from the reference program's by a relative error of at most 0.02.
Values may be sent and summed in bfloat16 or wider, within the bound.
A program may use at most 128 MiB of HBM per device.

```python
import jax
import jax.numpy as jnp
from jax import lax

D = 4608
QH = 32
KVH = 16
HD = 128
REQS = 12
NEWTOK = 192
SLOT_DEV = 1024
TOKENS = 2304
SLOTS = 16384
LONG = 5120
SHORT_MAX = 256
N_GY = 2


def pool_layout(key):
    base_key = jax.random.fold_in(key, 7)
    key_pick, key_short, key_trim, key_fresh, key_order, key_lead = jax.random.split(base_key, 6)
    picked = jax.random.permutation(key_pick, REQS)
    ident = jnp.arange(REQS, dtype=jnp.int32)
    lengths = jax.random.randint(key_short, (REQS,), 1, SHORT_MAX + 1)
    lengths = jnp.where(ident == picked[0], LONG, lengths)
    trimmed = LONG - jax.random.randint(key_trim, (), 0, NEWTOK)
    lengths = jnp.where(ident == picked[1], trimmed, lengths)
    lengths = jnp.where(ident == picked[3], 1, lengths).astype(jnp.int32)
    fresh = jax.random.randint(key_fresh, (REQS,), max(1, NEWTOK // 4), NEWTOK + 1)
    fresh = jnp.where(ident == picked[2], NEWTOK, fresh).astype(jnp.int32)
    scores = jax.random.permutation(key_order, REQS).astype(jnp.int32)
    scores = jnp.where(ident == picked[3], REQS, scores)
    ordering = jnp.argsort(scores, stable=True)
    spans = (lengths + NEWTOK)[ordering]
    starts = jnp.cumsum(spans) - spans
    slack = SLOTS - jnp.sum(spans)
    gap_at = jax.random.randint(key_lead, (), 1, REQS)
    shifted = starts + jnp.where(ident >= gap_at, slack, 0)
    offsets = jnp.zeros((REQS,), jnp.int32).at[ordering].set(shifted.astype(jnp.int32))
    return (lengths, fresh, offsets)


def draw_cached_len(key, part):
    return pool_layout(key)[0]


def draw_new_len(key, part):
    return pool_layout(key)[1]


def draw_slot_offset(key, part):
    return pool_layout(key)[2]


def draw_w_o(key, part):
    row_count = QH * HD
    key_entries, key_column = jax.random.split(jax.random.fold_in(key, 11))
    entries = jnp.clip(jax.random.normal(key_entries, (row_count, D), jnp.float32), -6.0, 6.0)
    column = jnp.clip(jax.random.normal(key_column, (D,), jnp.float32), -4.0, 4.0)
    strength = 1.5
    shaped = entries * row_count ** (-0.5) + strength * column[None, :] / row_count
    return shaped.astype(jnp.bfloat16)


def draw_v_cache(key, part):
    key_values = jax.random.fold_in(key, 13)
    values = jnp.clip(jax.random.normal(key_values, (SLOTS, KVH * HD), jnp.float32), -6.0, 6.0)
    offset_mean = 0.02
    return (values + offset_mean).astype(jnp.bfloat16)


def level_of(own_key, shape, pieces, low, top_value):
    def one(axis_at, blocks):
        heights = jax.random.uniform(jax.random.fold_in(jax.random.fold_in(own_key, 6), axis_at), (blocks,), jnp.float32, low / len(pieces), top_value / len(pieces))
        return jnp.repeat(jnp.exp(heights), shape[axis_at] // blocks).reshape((-1,) + (1,) * (len(shape) - axis_at - 1))

    gain = one(*pieces[0])
    for cut in pieces[1:]:
        gain = gain * one(*cut)
    return gain


def centred(rng, extent, width, limit, cuts=(), held_as=jnp.bfloat16):
    values = jax.random.normal(rng, extent, jnp.float32) * width
    if len(cuts) > 0:
        values = level_of(rng, extent, cuts, -0.22, 0.18) * values
    return jnp.clip(values, min=-limit, max=limit).astype(held_as)


def setup_inputs(seed: int = 0) -> dict:
    splits = jax.random.split(jax.random.key(seed), 13)
    tokens = centred(splits[0], (TOKENS, D), 1.0, 6.0, ((0, 16), (1, 2)))
    pre_gain = jnp.clip(jax.random.uniform(splits[1], (D,), jnp.float32, -0.5, 0.5) * level_of(splits[1], (D,), ((0, 2),), -0.4, 0.0), -0.5, 0.5).astype(jnp.bfloat16)
    w_q = centred(splits[2], (D, QH * HD), D ** -0.5, 0.09375, ((0, 16), (1, 2)))
    w_k = centred(splits[3], (D, KVH * HD), D ** -0.5, 0.09375, ((0, 16), (1, 2)))
    w_v = centred(splits[4], (D, KVH * HD), D ** -0.5, 0.09375, ((0, 16), (1, 2)))
    w_o = draw_w_o(jax.random.fold_in(splits[12], 71), 0)
    post_gain = jnp.clip(jax.random.uniform(splits[6], (D,), jnp.float32, -0.5, 0.5) * level_of(splits[6], (D,), ((0, 2),), -0.4, 0.0), -0.5, 0.5).astype(jnp.bfloat16)
    k_cache = centred(splits[7], (SLOTS, KVH * HD), 1.0, 6.0, ((0, 16), (1, 2)))
    v_cache = draw_v_cache(jax.random.fold_in(splits[12], 71), 0)
    cached_len = draw_cached_len(jax.random.fold_in(splits[12], 71), 0)
    new_len = draw_new_len(jax.random.fold_in(splits[12], 71), 0)
    slot_offset = draw_slot_offset(jax.random.fold_in(splits[12], 71), 0)
    return dict(tokens=tokens, pre_gain=pre_gain, w_q=w_q, w_k=w_k, w_v=w_v, w_o=w_o, post_gain=post_gain, k_cache=k_cache, v_cache=v_cache, cached_len=cached_len, new_len=new_len, slot_offset=slot_offset)


epsilon = 1e-06
soft_cap = 50.0
query_scale = 144.0 ** (-0.5)

def rotate(values, position, head_size):
    rows = values.shape[0]
    parts = values.reshape(rows, -1, head_size)
    half = head_size // 2
    inverse = jnp.power(10000.0, -2.0 * jnp.arange(half, dtype=jnp.float32) / head_size)
    angle = position.astype(jnp.float32)[:, None] * inverse[None, :]
    cosine = jnp.cos(angle)[:, None, :]
    sine = jnp.sin(angle)[:, None, :]
    first = parts[:, :, :half]
    second = parts[:, :, half:]
    turned = jnp.concatenate([first * cosine - second * sine, second * cosine + first * sine], axis=2)
    return turned.reshape(rows, -1)

def reference(tokens, pre_gain, w_q, w_k, w_v, w_o, post_gain, k_cache, v_cache, cached_len, new_len, slot_offset):
    float_in = tokens.astype(jnp.float32)
    scale_rows = lax.rsqrt(lax.optimization_barrier(jnp.mean(float_in * float_in, axis=1, keepdims=True)) + epsilon)
    normed = (float_in * scale_rows * (1.0 + pre_gain.astype(jnp.float32))).astype(jnp.bfloat16)
    q_lin = jnp.dot(normed, w_q, preferred_element_type=jnp.float32)
    k_lin = jnp.dot(normed, w_k, preferred_element_type=jnp.float32)
    v_lin = jnp.dot(normed, w_v, preferred_element_type=jnp.float32)
    row_ids = jnp.arange(TOKENS, dtype=jnp.int32)
    request = row_ids // NEWTOK
    within = row_ids % NEWTOK
    position = cached_len[request] + within
    queries = (rotate(q_lin, position, HD) * query_scale).astype(jnp.bfloat16)
    k_new = rotate(k_lin, position, HD).astype(jnp.bfloat16)
    v_new = v_lin.astype(jnp.bfloat16)
    target = jnp.where(within < new_len[request], slot_offset[request] + cached_len[request] + within, SLOTS)
    k_pool = k_cache.at[target].set(k_new, mode='drop')
    v_pool = v_cache.at[target].set(v_new, mode='drop')
    group_size = QH // KVH

    def attend_request(request_id):
        rows = lax.dynamic_slice_in_dim(queries, request_id * NEWTOK, NEWTOK, 0).astype(jnp.float32)
        rows = rows.reshape(NEWTOK, KVH, group_size, HD)
        offset = slot_offset[request_id]
        cached = cached_len[request_id]
        fresh_count = new_len[request_id]
        last_seen = cached + jnp.minimum(jnp.arange(NEWTOK, dtype=jnp.int32), fresh_count - 1)
        first_block = offset // SLOT_DEV
        final_block = (offset + cached + fresh_count - 1) // SLOT_DEV

        def block_terms(block, running):
            numerator, denominator = running
            key_rows = lax.dynamic_slice_in_dim(k_pool, block * SLOT_DEV, SLOT_DEV, 0).astype(jnp.float32)
            key_rows = key_rows.reshape(SLOT_DEV, KVH, HD)
            value_rows = lax.dynamic_slice_in_dim(v_pool, block * SLOT_DEV, SLOT_DEV, 0).astype(jnp.float32)
            value_rows = value_rows.reshape(SLOT_DEV, KVH, HD)
            key_pos = block * SLOT_DEV + jnp.arange(SLOT_DEV, dtype=jnp.int32) - offset
            visible = (key_pos[None, :] >= 0) & (key_pos[None, :] <= last_seen[:, None])
            logits = jnp.einsum('cgjd,sgd->cgjs', rows, key_rows)
            weight = jnp.where(visible[:, None, None, :], jnp.exp(soft_cap * jnp.tanh(logits / soft_cap)), 0.0)
            part_den = lax.optimization_barrier(jnp.sum(weight, axis=3)).astype(jnp.bfloat16)
            rounded = lax.optimization_barrier(weight.astype(jnp.bfloat16)).astype(jnp.float32)
            part_num = jnp.einsum('cgjs,sgd->cgjd', rounded, value_rows).astype(jnp.bfloat16)
            part_num, part_den = lax.optimization_barrier((part_num, part_den))
            return (numerator + part_num.astype(jnp.float32), denominator + part_den.astype(jnp.float32))
        initial = (jnp.zeros((NEWTOK, KVH, group_size, HD), jnp.float32), jnp.zeros((NEWTOK, KVH, group_size), jnp.float32))
        numerator, denominator = lax.fori_loop(first_block, final_block + 1, block_terms, initial)
        result = numerator / denominator[:, :, :, None]
        real_rows = jnp.arange(NEWTOK, dtype=jnp.int32) < fresh_count
        result = jnp.where(real_rows[:, None, None, None], result, 0.0)
        return result.reshape(NEWTOK, QH * HD).astype(jnp.bfloat16)
    attended = lax.map(attend_request, jnp.arange(REQS, dtype=jnp.int32)).reshape(TOKENS, QH * HD)
    group_cols = QH * HD // N_GY

    def add_group(group, summed):
        left = lax.dynamic_slice_in_dim(attended, group * group_cols, group_cols, 1)
        right = lax.dynamic_slice_in_dim(w_o, group * group_cols, group_cols, 0)
        part = jnp.dot(left, right, preferred_element_type=jnp.float32).astype(jnp.bfloat16)
        part = lax.optimization_barrier(part)
        return summed + part.astype(jnp.float32)
    branch = lax.fori_loop(0, N_GY, add_group, jnp.zeros((TOKENS, D), jnp.float32))
    mean_square = lax.optimization_barrier(jnp.mean(branch * branch, axis=1, keepdims=True))
    layer_out = (float_in + branch * lax.rsqrt(mean_square + epsilon) * (1.0 + post_gain.astype(jnp.float32))).astype(jnp.bfloat16)
    return (layer_out, k_pool, v_pool)
```

```python
import functools

import jax
import jax.numpy as jnp
from jax import lax
from jax.experimental import pallas as pl
from jax.experimental.pallas import tpu as pltpu
from jax.sharding import PartitionSpec as P

D = 4608
HD = 128
REQS = 12
NEWTOK = 192
KB = 256
VMEM_LIMIT = 56 * 1024 * 1024


epsilon = 1e-06
soft_cap = 50.0
query_scale = 144.0 ** (-0.5)


def project_kernel(q_blocks, rope_blocks, x_ref, w_ref, cos_ref, sin_ref, out_ref):
    block = pl.program_id(0)
    lin = jnp.dot(x_ref[...], w_ref[...], preferred_element_type=jnp.float32)
    heads = lin.shape[1] // HD

    @pl.when(block < rope_blocks)
    def _():
        scale = jnp.where(block < q_blocks, query_scale, 1.0)
        cosine = cos_ref[...] * scale
        sine = sin_ref[...] * scale
        for h in range(heads):
            u = lin[:, h * HD : (h + 1) * HD]
            swapped = pltpu.roll(u, HD // 2, 1)
            out_ref[:, h * HD : (h + 1) * HD] = (u * cosine + swapped * sine).astype(
                out_ref.dtype
            )

    @pl.when(block >= rope_blocks)
    def _():
        out_ref[...] = lin.astype(out_ref.dtype)


def project(normed, weights, cosine, sine, q_cols, rope_cols):
    rows, cols = normed.shape[0], weights.shape[1]
    width = min(512, cols - rope_cols)
    return pl.pallas_call(
        functools.partial(project_kernel, q_cols // width, rope_cols // width),
        grid=(cols // width,),
        in_specs=[
            pl.BlockSpec((rows, D), lambda i: (0, 0)),
            pl.BlockSpec((D, width), lambda i: (0, i)),
            pl.BlockSpec((rows, HD), lambda i: (0, 0)),
            pl.BlockSpec((rows, HD), lambda i: (0, 0)),
        ],
        out_specs=pl.BlockSpec((rows, width), lambda i: (0, i)),
        out_shape=jax.ShapeDtypeStruct((rows, cols), jnp.bfloat16),
        compiler_params=pltpu.CompilerParams(vmem_limit_bytes=VMEM_LIMIT),
        cost_estimate=pl.CostEstimate(
            flops=2 * rows * D * cols, bytes_accessed=2 * D * cols, transcendentals=0
        ),
    )(normed, weights, cosine, sine)


def attend_kernel(
    group, slab, info_ref, q_ref, k_ref, v_ref, kc_ref, vc_ref, kp_ref, vp_ref, nd_ref, acc_ref
):
    head = pl.program_id(0)
    gw = group * HD
    rows = group * NEWTOK
    den_at = nd_ref.shape[1] - HD
    kp_ref[...] = kc_ref[...]
    vp_ref[...] = vc_ref[...]
    num_cols = pl.ds(pl.multiple_of(head * gw, HD), gw)
    nd_ref[:, num_cols] = jnp.zeros((nd_ref.shape[0], gw), nd_ref.dtype)

    @pl.when(head == 0)
    def _():
        nd_ref[:, den_at:] = jnp.zeros((nd_ref.shape[0], HD), nd_ref.dtype)

    first = info_ref[3, 0]

    def request(r, carry):
        start = info_ref[2, r] - first
        cached = info_ref[0, r]
        fresh = info_ref[1, r]
        land = start + cached
        stop = land + fresh
        b_first = jnp.maximum(start, 0) // KB
        b_stop = (jnp.clip(stop, 0, slab) + (KB - 1)) // KB
        l_first = jnp.maximum(land, 0) // KB
        row0 = pl.multiple_of(r * NEWTOK, NEWTOK)

        @pl.when(b_stop > b_first)
        def _():
            def write(j, c):
                base = pl.multiple_of(j * KB, KB)
                at = lax.broadcasted_iota(jnp.int32, (KB, NEWTOK), 0) + (base - land)
                col = lax.broadcasted_iota(jnp.int32, (KB, NEWTOK), 1)
                pick = jnp.where((at == col) & (col < fresh), 1.0, 0.0).astype(jnp.bfloat16)
                here = lax.broadcasted_iota(jnp.int32, (KB, HD), 0) + (base - land)
                new = (here >= 0) & (here < fresh)
                for src, dst in ((k_ref, kp_ref), (v_ref, vp_ref)):
                    got = jnp.dot(
                        pick, src[pl.ds(row0, NEWTOK), :], preferred_element_type=jnp.float32
                    )
                    old = dst[pl.ds(base, KB), :].astype(jnp.float32)
                    dst[pl.ds(base, KB), :] = jnp.where(new, got, old).astype(dst.dtype)
                return c

            lax.fori_loop(l_first, b_stop, write, 0)

            acc_ref[...] = jnp.zeros_like(acc_ref)
            q = jnp.concatenate(
                [q_ref[pl.ds(row0, NEWTOK), g * HD : (g + 1) * HD] for g in range(group)], axis=0
            )
            ones = jnp.ones((KB, HD), jnp.bfloat16)
            index = lax.broadcasted_iota(jnp.int32, (rows, KB), 0) % NEWTOK
            last = cached + jnp.minimum(index, fresh - 1)
            slot = lax.broadcasted_iota(jnp.int32, (rows, KB), 1)

            def block(j, c):
                base = pl.multiple_of(j * KB, KB)
                logits = lax.dot_general(
                    q,
                    kp_ref[pl.ds(base, KB), :],
                    (((1,), (1,)), ((), ())),
                    preferred_element_type=jnp.float32,
                )
                weight = jnp.exp(soft_cap * jnp.tanh(logits * (1.0 / soft_cap)))
                at = slot + (base - start)
                weight = jnp.where((at >= 0) & (at <= last), weight, 0.0).astype(jnp.bfloat16)
                values = jnp.concatenate([vp_ref[pl.ds(base, KB), :], ones], axis=1)
                acc_ref[...] += jnp.dot(weight, values, preferred_element_type=jnp.float32)
                return c

            lax.fori_loop(b_first, b_stop, block, 0)
            for g in range(group):
                nd_ref[
                    pl.ds(row0, NEWTOK), pl.ds(pl.multiple_of(head * gw + g * HD, HD), HD)
                ] = acc_ref[g * NEWTOK : (g + 1) * NEWTOK, :HD].astype(nd_ref.dtype)
            lane = lax.broadcasted_iota(jnp.int32, (NEWTOK, HD), 1)
            den = nd_ref[pl.ds(row0, NEWTOK), den_at:].astype(jnp.float32)
            for g in range(group):
                den = jnp.where(
                    lane == head * group + g, acc_ref[g * NEWTOK : (g + 1) * NEWTOK, HD:], den
                )
            nd_ref[pl.ds(row0, NEWTOK), den_at:] = den.astype(nd_ref.dtype)

        return carry

    lax.fori_loop(0, REQS, request, 0)


def attend(info, qkv, k_cache, v_cache):
    slab, kv_cols = k_cache.shape
    total = qkv.shape[0]
    kv = kv_cols // HD
    q_cols = qkv.shape[1] - 2 * kv_cols
    group = q_cols // kv_cols
    pool = pl.BlockSpec((slab, HD), lambda c: (0, c))
    return pl.pallas_call(
        functools.partial(attend_kernel, group, slab),
        grid=(kv,),
        in_specs=[
            pl.BlockSpec(memory_space=pltpu.SMEM),
            pl.BlockSpec((total, group * HD), lambda c: (0, c)),
            pl.BlockSpec((total, HD), lambda c: (0, q_cols // HD + c)),
            pl.BlockSpec((total, HD), lambda c: (0, (q_cols + kv_cols) // HD + c)),
            pool,
            pool,
        ],
        out_specs=[
            pool,
            pool,
            pl.BlockSpec((total, q_cols + HD), lambda c: (0, 0)),
        ],
        out_shape=[
            jax.ShapeDtypeStruct(k_cache.shape, k_cache.dtype),
            jax.ShapeDtypeStruct(v_cache.shape, v_cache.dtype),
            jax.ShapeDtypeStruct((total, q_cols + HD), jnp.bfloat16),
        ],
        scratch_shapes=[pltpu.VMEM((group * NEWTOK, 2 * HD), jnp.float32)],
        compiler_params=pltpu.CompilerParams(vmem_limit_bytes=VMEM_LIMIT),
        cost_estimate=pl.CostEstimate(
            flops=4 * 2 * NEWTOK * slab * q_cols * 2,
            bytes_accessed=2 * total * (2 * q_cols + 2 * kv_cols),
            transcendentals=4 * NEWTOK * slab * q_cols // HD,
        ),
    )(info, qkv, qkv, qkv, k_cache, v_cache)


def on_device(
    tokens,
    pre_gain,
    w_q,
    w_k,
    w_v,
    w_o,
    post_gain,
    k_cache,
    v_cache,
    cached_len,
    new_len,
    slot_offset,
):
    tok_rows = tokens.shape[0]
    q_cols, kv_cols = w_q.shape[1], w_k.shape[1]
    n_gy = D // tokens.shape[1]
    gy = lax.axis_index("gy")
    weights = lax.all_gather(jnp.concatenate([w_q, w_k, w_v], axis=1), "gx", axis=0, tiled=True)
    if n_gy == 2:
        swap = [(0, 1), (1, 0)]
        other_in = lax.ppermute(tokens, "gy", swap)
        other_gain = lax.ppermute(pre_gain, "gy", swap)
        whole_in = jnp.where(
            gy == 0,
            jnp.concatenate([tokens, other_in], axis=1),
            jnp.concatenate([other_in, tokens], axis=1),
        )
        whole_gain = jnp.where(
            gy == 0,
            jnp.concatenate([pre_gain, other_gain]),
            jnp.concatenate([other_gain, pre_gain]),
        )
    else:
        whole_in = lax.all_gather(tokens, "gy", axis=1, tiled=True)
        whole_gain = lax.all_gather(pre_gain, "gy", axis=0, tiled=True)
    float_in = whole_in.astype(jnp.float32)
    scale_rows = lax.rsqrt(jnp.mean(float_in * float_in, axis=1, keepdims=True) + epsilon)
    normed = (float_in * scale_rows * (1.0 + whole_gain.astype(jnp.float32))).astype(jnp.bfloat16)
    row_ids = lax.axis_index("gx") * tok_rows + jnp.arange(tok_rows, dtype=jnp.int32)
    request = row_ids // NEWTOK
    within = row_ids % NEWTOK
    owner_mask = request[:, None] == jnp.arange(REQS, dtype=jnp.int32)[None, :]
    row_cached = jnp.sum(jnp.where(owner_mask, cached_len[None, :], 0), axis=1)
    row_fresh = jnp.sum(jnp.where(owner_mask, new_len[None, :], 0), axis=1)
    position = row_cached + within
    half = HD // 2
    inverse = jnp.power(10000.0, -2.0 * jnp.arange(half, dtype=jnp.float32) / HD)
    angle = position.astype(jnp.float32)[:, None] * inverse[None, :]
    cosine, sine = jnp.cos(angle), jnp.sin(angle)
    cosine = jnp.concatenate([cosine, cosine], axis=1)
    sine = jnp.concatenate([-sine, sine], axis=1)
    qkv_new = project(normed, weights, cosine, sine, q_cols, q_cols + kv_cols)
    qkv = lax.all_gather(qkv_new, "gx", axis=0, tiled=True)
    qkv, w_o = lax.optimization_barrier((qkv, w_o))
    w_out = lax.all_gather(w_o, "gx", axis=1, tiled=True)
    slab = k_cache.shape[0]
    first = jnp.full((REQS,), lax.axis_index("gx") * slab, jnp.int32)
    info = jnp.stack([cached_len, new_len, slot_offset, first])
    k_pool, v_pool, num_den = attend(info, qkv, k_cache, v_cache)
    sums = lax.psum_scatter(num_den, "gx", scatter_dimension=0, tiled=True).astype(jnp.float32)
    heads = q_cols // HD
    head_num = sums[:, :q_cols].reshape(tok_rows, heads, HD)
    head_den = sums[:, q_cols : q_cols + heads]
    attended = head_num / head_den[:, :, None]
    attended = jnp.where((within < row_fresh)[:, None, None], attended, 0.0)
    attended = attended.reshape(tok_rows, q_cols).astype(jnp.bfloat16)
    partial_out = jnp.dot(attended, w_out, preferred_element_type=jnp.float32).astype(jnp.bfloat16)
    if n_gy == 2:
        low, high = partial_out[:, : D // 2], partial_out[:, D // 2 :]
        theirs = lax.ppermute(jnp.where(gy == 0, high, low), "gy", swap)
        branch = jnp.where(gy == 0, low, high).astype(jnp.float32) + theirs.astype(jnp.float32)
        square = jnp.sum(branch * branch, axis=1)
        mean_square = (square + lax.ppermute(square, "gy", swap)) / D
    else:
        branch = lax.psum_scatter(partial_out, "gy", scatter_dimension=1, tiled=True).astype(
            jnp.float32
        )
        mean_square = lax.psum(jnp.sum(branch * branch, axis=1), "gy") / D
    layer_out = (
        tokens.astype(jnp.float32)
        + branch * lax.rsqrt(mean_square + epsilon)[:, None] * (1.0 + post_gain.astype(jnp.float32))
    ).astype(jnp.bfloat16)
    return (layer_out, k_pool, v_pool)


def solution(mesh):
    placed = (
        P("gx", "gy"),
        P("gy"),
        P("gx", "gy"),
        P("gx", "gy"),
        P("gx", "gy"),
        P("gy", "gx"),
        P("gy"),
        P("gx", "gy"),
        P("gx", "gy"),
        P(),
        P(),
        P(),
    )
    return jax.shard_map(
        on_device,
        mesh=mesh,
        in_specs=placed,
        out_specs=(P("gx", "gy"), P("gx", "gy"), P("gx", "gy")),
        check_vma=False,
    )
```

```python
import functools

import jax
import jax.numpy as jnp
from jax import lax
from jax.experimental import pallas as pl
from jax.experimental.pallas import tpu as pltpu
from jax.sharding import PartitionSpec as P

D = 4608
HD = 128
REQS = 12
NEWTOK = 192
KB = 256
VMEM_LIMIT = 56 * 1024 * 1024


epsilon = 1e-06
soft_cap = 50.0
query_scale = 144.0 ** (-0.5)


def project_kernel(q_blocks, rope_blocks, x_ref, w_ref, cos_ref, sin_ref, out_ref):
    block = pl.program_id(0)
    lin = jnp.dot(x_ref[...], w_ref[...], preferred_element_type=jnp.float32)
    heads = lin.shape[1] // HD

    @pl.when(block < rope_blocks)
    def _():
        scale = jnp.where(block < q_blocks, query_scale, 1.0)
        cosine = cos_ref[...] * scale
        sine = sin_ref[...] * scale
        for h in range(heads):
            u = lin[:, h * HD : (h + 1) * HD]
            swapped = pltpu.roll(u, HD // 2, 1)
            out_ref[:, h * HD : (h + 1) * HD] = (u * cosine + swapped * sine).astype(
                out_ref.dtype
            )

    @pl.when(block >= rope_blocks)
    def _():
        out_ref[...] = lin.astype(out_ref.dtype)


def project(normed, weights, cosine, sine, q_cols, rope_cols):
    rows, cols = normed.shape[0], weights.shape[1]
    width = min(512, cols - rope_cols)
    return pl.pallas_call(
        functools.partial(project_kernel, q_cols // width, rope_cols // width),
        grid=(cols // width,),
        in_specs=[
            pl.BlockSpec((rows, D), lambda i: (0, 0)),
            pl.BlockSpec((D, width), lambda i: (0, i)),
            pl.BlockSpec((rows, HD), lambda i: (0, 0)),
            pl.BlockSpec((rows, HD), lambda i: (0, 0)),
        ],
        out_specs=pl.BlockSpec((rows, width), lambda i: (0, i)),
        out_shape=jax.ShapeDtypeStruct((rows, cols), jnp.bfloat16),
        compiler_params=pltpu.CompilerParams(vmem_limit_bytes=VMEM_LIMIT),
        cost_estimate=pl.CostEstimate(
            flops=2 * rows * D * cols, bytes_accessed=2 * D * cols, transcendentals=0
        ),
    )(normed, weights, cosine, sine)


def attend_kernel(
    group, slab, info_ref, q_ref, k_ref, v_ref, kc_ref, vc_ref, kp_ref, vp_ref, nd_ref, acc_ref
):
    head = pl.program_id(0)
    gw = group * HD
    rows = group * NEWTOK
    den_at = nd_ref.shape[1] - HD
    kp_ref[...] = kc_ref[...]
    vp_ref[...] = vc_ref[...]
    num_cols = pl.ds(pl.multiple_of(head * gw, HD), gw)
    nd_ref[:, num_cols] = jnp.zeros((nd_ref.shape[0], gw), nd_ref.dtype)

    @pl.when(head == 0)
    def _():
        nd_ref[:, den_at:] = jnp.zeros((nd_ref.shape[0], HD), nd_ref.dtype)

    first = info_ref[3, 0]

    def request(r, carry):
        start = info_ref[2, r] - first
        cached = info_ref[0, r]
        fresh = info_ref[1, r]
        land = start + cached
        stop = land + fresh
        b_first = jnp.maximum(start, 0) // KB
        b_stop = (jnp.clip(stop, 0, slab) + (KB - 1)) // KB
        l_first = jnp.maximum(land, 0) // KB
        row0 = pl.multiple_of(r * NEWTOK, NEWTOK)

        @pl.when(b_stop > b_first)
        def _():
            def write(j, c):
                base = pl.multiple_of(j * KB, KB)
                at = lax.broadcasted_iota(jnp.int32, (KB, NEWTOK), 0) + (base - land)
                col = lax.broadcasted_iota(jnp.int32, (KB, NEWTOK), 1)
                pick = jnp.where((at == col) & (col < fresh), 1.0, 0.0).astype(jnp.bfloat16)
                here = lax.broadcasted_iota(jnp.int32, (KB, HD), 0) + (base - land)
                new = (here >= 0) & (here < fresh)
                for src, dst in ((k_ref, kp_ref), (v_ref, vp_ref)):
                    got = jnp.dot(
                        pick, src[pl.ds(row0, NEWTOK), :], preferred_element_type=jnp.float32
                    )
                    old = dst[pl.ds(base, KB), :].astype(jnp.float32)
                    dst[pl.ds(base, KB), :] = jnp.where(new, got, old).astype(dst.dtype)
                return c

            lax.fori_loop(l_first, b_stop, write, 0)

            acc_ref[...] = jnp.zeros_like(acc_ref)
            q = jnp.concatenate(
                [q_ref[pl.ds(row0, NEWTOK), g * HD : (g + 1) * HD] for g in range(group)], axis=0
            )
            ones = jnp.ones((KB, HD), jnp.bfloat16)
            index = lax.broadcasted_iota(jnp.int32, (rows, KB), 0) % NEWTOK
            last = cached + jnp.minimum(index, fresh - 1)
            slot = lax.broadcasted_iota(jnp.int32, (rows, KB), 1)

            def block(j, c):
                base = pl.multiple_of(j * KB, KB)
                logits = lax.dot_general(
                    q,
                    kp_ref[pl.ds(base, KB), :],
                    (((1,), (1,)), ((), ())),
                    preferred_element_type=jnp.float32,
                )
                weight = jnp.exp(soft_cap * jnp.tanh(logits * (1.0 / soft_cap)))
                at = slot + (base - start)
                weight = jnp.where((at >= 0) & (at <= last), weight, 0.0).astype(jnp.bfloat16)
                values = jnp.concatenate([vp_ref[pl.ds(base, KB), :], ones], axis=1)
                acc_ref[...] += jnp.dot(weight, values, preferred_element_type=jnp.float32)
                return c

            lax.fori_loop(b_first, b_stop, block, 0)
            for g in range(group):
                nd_ref[
                    pl.ds(row0, NEWTOK), pl.ds(pl.multiple_of(head * gw + g * HD, HD), HD)
                ] = acc_ref[g * NEWTOK : (g + 1) * NEWTOK, :HD].astype(nd_ref.dtype)
            lane = lax.broadcasted_iota(jnp.int32, (NEWTOK, HD), 1)
            den = nd_ref[pl.ds(row0, NEWTOK), den_at:].astype(jnp.float32)
            for g in range(group):
                den = jnp.where(
                    lane == head * group + g, acc_ref[g * NEWTOK : (g + 1) * NEWTOK, HD:], den
                )
            nd_ref[pl.ds(row0, NEWTOK), den_at:] = den.astype(nd_ref.dtype)

        return carry

    lax.fori_loop(0, REQS, request, 0)


def attend(info, qkv, k_cache, v_cache):
    slab, kv_cols = k_cache.shape
    total = qkv.shape[0]
    kv = kv_cols // HD
    q_cols = qkv.shape[1] - 2 * kv_cols
    group = q_cols // kv_cols
    pool = pl.BlockSpec((slab, HD), lambda c: (0, c))
    return pl.pallas_call(
        functools.partial(attend_kernel, group, slab),
        grid=(kv,),
        in_specs=[
            pl.BlockSpec(memory_space=pltpu.SMEM),
            pl.BlockSpec((total, group * HD), lambda c: (0, c)),
            pl.BlockSpec((total, HD), lambda c: (0, q_cols // HD + c)),
            pl.BlockSpec((total, HD), lambda c: (0, (q_cols + kv_cols) // HD + c)),
            pool,
            pool,
        ],
        out_specs=[
            pool,
            pool,
            pl.BlockSpec((total, q_cols + HD), lambda c: (0, 0)),
        ],
        out_shape=[
            jax.ShapeDtypeStruct(k_cache.shape, k_cache.dtype),
            jax.ShapeDtypeStruct(v_cache.shape, v_cache.dtype),
            jax.ShapeDtypeStruct((total, q_cols + HD), jnp.bfloat16),
        ],
        scratch_shapes=[pltpu.VMEM((group * NEWTOK, 2 * HD), jnp.float32)],
        compiler_params=pltpu.CompilerParams(vmem_limit_bytes=VMEM_LIMIT),
        cost_estimate=pl.CostEstimate(
            flops=4 * 2 * NEWTOK * slab * q_cols * 2,
            bytes_accessed=2 * total * (2 * q_cols + 2 * kv_cols),
            transcendentals=4 * NEWTOK * slab * q_cols // HD,
        ),
    )(info, qkv, qkv, qkv, k_cache, v_cache)


def out_kernel(half_ref, x_ref, w_ref, out_ref):
    out_ref[...] = lax.dot_general(
        x_ref[...], w_ref[...], (((1,), (1,)), ((), ())), preferred_element_type=jnp.float32
    ).astype(out_ref.dtype)


def out_half(attended, w_out, half):
    rows, depth = attended.shape
    cols = w_out.shape[0] // 2
    width = 384
    steps = cols // width
    return pl.pallas_call(
        out_kernel,
        grid_spec=pltpu.PrefetchScalarGridSpec(
            num_scalar_prefetch=1,
            grid=(steps,),
            in_specs=[
                pl.BlockSpec((rows, depth), lambda i, half: (0, 0)),
                pl.BlockSpec((width, depth), lambda i, half: (half[0] * steps + i, 0)),
            ],
            out_specs=pl.BlockSpec((rows, width), lambda i, half: (0, i)),
        ),
        out_shape=jax.ShapeDtypeStruct((rows, cols), jnp.bfloat16),
        compiler_params=pltpu.CompilerParams(vmem_limit_bytes=VMEM_LIMIT),
        cost_estimate=pl.CostEstimate(
            flops=2 * rows * depth * cols, bytes_accessed=2 * depth * cols, transcendentals=0
        ),
    )(half.reshape(1).astype(jnp.int32), attended, w_out)


def on_device(
    tokens,
    pre_gain,
    w_q,
    w_k,
    w_v,
    w_o,
    post_gain,
    k_cache,
    v_cache,
    cached_len,
    new_len,
    slot_offset,
):
    tok_rows = tokens.shape[0]
    q_cols, kv_cols = w_q.shape[1], w_k.shape[1]
    n_gy = D // tokens.shape[1]
    gy = lax.axis_index("gy")
    weights = lax.all_gather(jnp.concatenate([w_q, w_k, w_v], axis=1), "gx", axis=0, tiled=True)
    if n_gy == 2:
        swap = [(0, 1), (1, 0)]
        other_in = lax.ppermute(tokens, "gy", swap)
        other_gain = lax.ppermute(pre_gain, "gy", swap)
        whole_in = jnp.where(
            gy == 0,
            jnp.concatenate([tokens, other_in], axis=1),
            jnp.concatenate([other_in, tokens], axis=1),
        )
        whole_gain = jnp.where(
            gy == 0,
            jnp.concatenate([pre_gain, other_gain]),
            jnp.concatenate([other_gain, pre_gain]),
        )
    else:
        whole_in = lax.all_gather(tokens, "gy", axis=1, tiled=True)
        whole_gain = lax.all_gather(pre_gain, "gy", axis=0, tiled=True)
    float_in = whole_in.astype(jnp.float32)
    scale_rows = lax.rsqrt(jnp.mean(float_in * float_in, axis=1, keepdims=True) + epsilon)
    normed = (float_in * scale_rows * (1.0 + whole_gain.astype(jnp.float32))).astype(jnp.bfloat16)
    row_ids = lax.axis_index("gx") * tok_rows + jnp.arange(tok_rows, dtype=jnp.int32)
    request = row_ids // NEWTOK
    within = row_ids % NEWTOK
    owner_mask = request[:, None] == jnp.arange(REQS, dtype=jnp.int32)[None, :]
    row_cached = jnp.sum(jnp.where(owner_mask, cached_len[None, :], 0), axis=1)
    row_fresh = jnp.sum(jnp.where(owner_mask, new_len[None, :], 0), axis=1)
    position = row_cached + within
    half = HD // 2
    inverse = jnp.power(10000.0, -2.0 * jnp.arange(half, dtype=jnp.float32) / HD)
    angle = position.astype(jnp.float32)[:, None] * inverse[None, :]
    cosine, sine = jnp.cos(angle), jnp.sin(angle)
    cosine = jnp.concatenate([cosine, cosine], axis=1)
    sine = jnp.concatenate([-sine, sine], axis=1)
    qkv_new = project(normed, weights, cosine, sine, q_cols, q_cols + kv_cols)
    qkv = lax.all_gather(qkv_new, "gx", axis=0, tiled=True)
    qkv, w_o_t = lax.optimization_barrier((qkv, w_o.T))
    w_out = lax.all_gather(w_o_t, "gx", axis=0, tiled=True)
    slab = k_cache.shape[0]
    first = jnp.full((REQS,), lax.axis_index("gx") * slab, jnp.int32)
    info = jnp.stack([cached_len, new_len, slot_offset, first])
    k_pool, v_pool, num_den = attend(info, qkv, k_cache, v_cache)
    n_gx = num_den.shape[0] // tok_rows
    core = lax.axis_index("gx") % 2
    halves = num_den.reshape(n_gx // 2, 2, tok_rows, num_den.shape[1])
    kept = jnp.where(core == 0, halves[:, 0], halves[:, 1])
    given = jnp.where(core == 0, halves[:, 1], halves[:, 0])
    taken = lax.ppermute(given, "gx", [(i, i ^ 1) for i in range(n_gx)])
    chip = (kept.astype(jnp.float32) + taken.astype(jnp.float32)).astype(jnp.bfloat16)
    chip, w_out = lax.optimization_barrier((chip, w_out))
    sums = lax.psum_scatter(
        chip.reshape(n_gx // 2 * tok_rows, num_den.shape[1]),
        "gx",
        scatter_dimension=0,
        axis_index_groups=[list(range(c, n_gx, 2)) for c in range(2)],
        tiled=True,
    ).astype(jnp.float32)
    heads = q_cols // HD
    head_num = sums[:, :q_cols].reshape(tok_rows, heads, HD)
    head_den = sums[:, q_cols : q_cols + heads]
    attended = head_num / head_den[:, :, None]
    attended = jnp.where((within < row_fresh)[:, None, None], attended, 0.0)
    attended = attended.reshape(tok_rows, q_cols).astype(jnp.bfloat16)
    if n_gy == 2:
        theirs = lax.ppermute(out_half(attended, w_out, 1 - gy), "gy", swap)
        own = out_half(attended, w_out, gy)
        branch = own.astype(jnp.float32) + theirs.astype(jnp.float32)
        square = jnp.sum(branch * branch, axis=1)
        mean_square = (square + lax.ppermute(square, "gy", swap)) / D
    else:
        partial_out = lax.dot_general(
            attended, w_out, (((1,), (1,)), ((), ())), preferred_element_type=jnp.float32
        ).astype(jnp.bfloat16)
        branch = lax.psum_scatter(partial_out, "gy", scatter_dimension=1, tiled=True).astype(
            jnp.float32
        )
        mean_square = lax.psum(jnp.sum(branch * branch, axis=1), "gy") / D
    layer_out = (
        tokens.astype(jnp.float32)
        + branch * lax.rsqrt(mean_square + epsilon)[:, None] * (1.0 + post_gain.astype(jnp.float32))
    ).astype(jnp.bfloat16)
    return (layer_out, k_pool, v_pool)


def solution(mesh):
    placed = (
        P("gx", "gy"),
        P("gy"),
        P("gx", "gy"),
        P("gx", "gy"),
        P("gx", "gy"),
        P("gy", "gx"),
        P("gy"),
        P("gx", "gy"),
        P("gx", "gy"),
        P(),
        P(),
        P(),
    )
    return jax.shard_map(
        on_device,
        mesh=mesh,
        in_specs=placed,
        out_specs=(P("gx", "gy"), P("gx", "gy"), P("gx", "gy")),
        check_vma=False,
    )
```

```python
import functools

import jax
import jax.numpy as jnp
from jax import lax
from jax.experimental import pallas as pl
from jax.experimental.pallas import tpu as pltpu
from jax.sharding import PartitionSpec as P

D = 4608
HD = 128
REQS = 12
NEWTOK = 192
KB = 256
VMEM_LIMIT = 56 * 1024 * 1024


epsilon = 1e-06
soft_cap = 50.0
query_scale = 144.0 ** (-0.5)


def project_kernel(q_blocks, rope_blocks, x_ref, w_ref, cos_ref, sin_ref, out_ref):
    block = pl.program_id(0)
    lin = jnp.dot(x_ref[...], w_ref[...], preferred_element_type=jnp.float32)
    heads = lin.shape[1] // HD

    @pl.when(block < rope_blocks)
    def _():
        scale = jnp.where(block < q_blocks, query_scale, 1.0)
        cosine = cos_ref[...] * scale
        sine = sin_ref[...] * scale
        for h in range(heads):
            u = lin[:, h * HD : (h + 1) * HD]
            swapped = pltpu.roll(u, HD // 2, 1)
            out_ref[:, h * HD : (h + 1) * HD] = (u * cosine + swapped * sine).astype(
                out_ref.dtype
            )

    @pl.when(block >= rope_blocks)
    def _():
        out_ref[...] = lin.astype(out_ref.dtype)


def project(normed, weights, cosine, sine, q_cols, rope_cols):
    rows, cols = normed.shape[0], weights.shape[1]
    width = min(512, cols - rope_cols)
    return pl.pallas_call(
        functools.partial(project_kernel, q_cols // width, rope_cols // width),
        grid=(cols // width,),
        in_specs=[
            pl.BlockSpec((rows, D), lambda i: (0, 0)),
            pl.BlockSpec((D, width), lambda i: (0, i)),
            pl.BlockSpec((rows, HD), lambda i: (0, 0)),
            pl.BlockSpec((rows, HD), lambda i: (0, 0)),
        ],
        out_specs=pl.BlockSpec((rows, width), lambda i: (0, i)),
        out_shape=jax.ShapeDtypeStruct((rows, cols), jnp.bfloat16),
        compiler_params=pltpu.CompilerParams(vmem_limit_bytes=VMEM_LIMIT),
        cost_estimate=pl.CostEstimate(
            flops=2 * rows * D * cols, bytes_accessed=2 * D * cols, transcendentals=0
        ),
    )(normed, weights, cosine, sine)


def attend_kernel(
    group, slab, info_ref, q_ref, k_ref, v_ref, kc_ref, vc_ref, kp_ref, vp_ref, nd_ref, acc_ref
):
    head = pl.program_id(0)
    gw = group * HD
    rows = group * NEWTOK
    den_at = nd_ref.shape[1] - HD
    kp_ref[...] = kc_ref[...]
    vp_ref[...] = vc_ref[...]
    num_cols = pl.ds(pl.multiple_of(head * gw, HD), gw)
    nd_ref[:, num_cols] = jnp.zeros((nd_ref.shape[0], gw), nd_ref.dtype)

    @pl.when(head == 0)
    def _():
        nd_ref[:, den_at:] = jnp.zeros((nd_ref.shape[0], HD), nd_ref.dtype)

    first = info_ref[3, 0]

    def request(r, carry):
        start = info_ref[2, r] - first
        cached = info_ref[0, r]
        fresh = info_ref[1, r]
        land = start + cached
        stop = land + fresh
        b_first = jnp.maximum(start, 0) // KB
        b_stop = (jnp.clip(stop, 0, slab) + (KB - 1)) // KB
        l_first = jnp.maximum(land, 0) // KB
        row0 = pl.multiple_of(r * NEWTOK, NEWTOK)

        @pl.when(b_stop > b_first)
        def _():
            def write(j, c):
                base = pl.multiple_of(j * KB, KB)
                at = lax.broadcasted_iota(jnp.int32, (KB, NEWTOK), 0) + (base - land)
                col = lax.broadcasted_iota(jnp.int32, (KB, NEWTOK), 1)
                pick = jnp.where((at == col) & (col < fresh), 1.0, 0.0).astype(jnp.bfloat16)
                here = lax.broadcasted_iota(jnp.int32, (KB, HD), 0) + (base - land)
                new = (here >= 0) & (here < fresh)
                for src, dst in ((k_ref, kp_ref), (v_ref, vp_ref)):
                    got = jnp.dot(
                        pick, src[pl.ds(row0, NEWTOK), :], preferred_element_type=jnp.float32
                    )
                    old = dst[pl.ds(base, KB), :].astype(jnp.float32)
                    dst[pl.ds(base, KB), :] = jnp.where(new, got, old).astype(dst.dtype)
                return c

            lax.fori_loop(l_first, b_stop, write, 0)

            acc_ref[...] = jnp.zeros_like(acc_ref)
            q = jnp.concatenate(
                [q_ref[pl.ds(row0, NEWTOK), g * HD : (g + 1) * HD] for g in range(group)], axis=0
            )
            ones = jnp.ones((KB, HD), jnp.bfloat16)
            index = lax.broadcasted_iota(jnp.int32, (rows, KB), 0) % NEWTOK
            last = cached + jnp.minimum(index, fresh - 1)
            slot = lax.broadcasted_iota(jnp.int32, (rows, KB), 1)

            def block(j, c):
                base = pl.multiple_of(j * KB, KB)
                logits = lax.dot_general(
                    q,
                    kp_ref[pl.ds(base, KB), :],
                    (((1,), (1,)), ((), ())),
                    preferred_element_type=jnp.float32,
                )
                weight = jnp.exp(soft_cap * jnp.tanh(logits * (1.0 / soft_cap)))
                at = slot + (base - start)
                weight = jnp.where((at >= 0) & (at <= last), weight, 0.0).astype(jnp.bfloat16)
                values = jnp.concatenate([vp_ref[pl.ds(base, KB), :], ones], axis=1)
                acc_ref[...] += jnp.dot(weight, values, preferred_element_type=jnp.float32)
                return c

            lax.fori_loop(b_first, b_stop, block, 0)
            for g in range(group):
                nd_ref[
                    pl.ds(row0, NEWTOK), pl.ds(pl.multiple_of(head * gw + g * HD, HD), HD)
                ] = acc_ref[g * NEWTOK : (g + 1) * NEWTOK, :HD].astype(nd_ref.dtype)
            lane = lax.broadcasted_iota(jnp.int32, (NEWTOK, HD), 1)
            den = nd_ref[pl.ds(row0, NEWTOK), den_at:].astype(jnp.float32)
            for g in range(group):
                den = jnp.where(
                    lane == head * group + g, acc_ref[g * NEWTOK : (g + 1) * NEWTOK, HD:], den
                )
            nd_ref[pl.ds(row0, NEWTOK), den_at:] = den.astype(nd_ref.dtype)

        return carry

    lax.fori_loop(0, REQS, request, 0)


def attend(info, qkv, k_cache, v_cache):
    slab, kv_cols = k_cache.shape
    total = qkv.shape[0]
    kv = kv_cols // HD
    q_cols = qkv.shape[1] - 2 * kv_cols
    group = q_cols // kv_cols
    pool = pl.BlockSpec((slab, HD), lambda c: (0, c))
    return pl.pallas_call(
        functools.partial(attend_kernel, group, slab),
        grid=(kv,),
        in_specs=[
            pl.BlockSpec(memory_space=pltpu.SMEM),
            pl.BlockSpec((total, group * HD), lambda c: (0, c)),
            pl.BlockSpec((total, HD), lambda c: (0, q_cols // HD + c)),
            pl.BlockSpec((total, HD), lambda c: (0, (q_cols + kv_cols) // HD + c)),
            pool,
            pool,
        ],
        out_specs=[
            pool,
            pool,
            pl.BlockSpec((total, q_cols + HD), lambda c: (0, 0)),
        ],
        out_shape=[
            jax.ShapeDtypeStruct(k_cache.shape, k_cache.dtype),
            jax.ShapeDtypeStruct(v_cache.shape, v_cache.dtype),
            jax.ShapeDtypeStruct((total, q_cols + HD), jnp.bfloat16),
        ],
        scratch_shapes=[pltpu.VMEM((group * NEWTOK, 2 * HD), jnp.float32)],
        compiler_params=pltpu.CompilerParams(vmem_limit_bytes=VMEM_LIMIT),
        cost_estimate=pl.CostEstimate(
            flops=4 * 2 * NEWTOK * slab * q_cols * 2,
            bytes_accessed=2 * total * (2 * q_cols + 2 * kv_cols),
            transcendentals=4 * NEWTOK * slab * q_cols // HD,
        ),
    )(info, qkv, qkv, qkv, k_cache, v_cache)


def out_kernel(half_ref, x_ref, w_ref, out_ref):
    out_ref[...] = lax.dot_general(
        x_ref[...], w_ref[...], (((1,), (1,)), ((), ())), preferred_element_type=jnp.float32
    ).astype(out_ref.dtype)


def out_half(attended, w_out, half):
    rows, depth = attended.shape
    cols = w_out.shape[0] // 2
    width = 384
    steps = cols // width
    return pl.pallas_call(
        out_kernel,
        grid_spec=pltpu.PrefetchScalarGridSpec(
            num_scalar_prefetch=1,
            grid=(steps,),
            in_specs=[
                pl.BlockSpec((rows, depth), lambda i, half: (0, 0)),
                pl.BlockSpec((width, depth), lambda i, half: (half[0] * steps + i, 0)),
            ],
            out_specs=pl.BlockSpec((rows, width), lambda i, half: (0, i)),
        ),
        out_shape=jax.ShapeDtypeStruct((rows, cols), jnp.bfloat16),
        compiler_params=pltpu.CompilerParams(vmem_limit_bytes=VMEM_LIMIT),
        cost_estimate=pl.CostEstimate(
            flops=2 * rows * depth * cols, bytes_accessed=2 * depth * cols, transcendentals=0
        ),
    )(half.reshape(1).astype(jnp.int32), attended, w_out)


def pair_sum(blocks, stride, count):
    side = lax.axis_index("gx") // stride % 2
    given = lax.dynamic_index_in_dim(blocks, 1 - side, 1, keepdims=False)
    taken = lax.ppermute(given, "gx", [(i, i ^ stride) for i in range(count)])
    kept = lax.dynamic_index_in_dim(blocks, side, 1, keepdims=False)
    return (kept.astype(jnp.float32) + taken.astype(jnp.float32)).astype(jnp.bfloat16)


def scatter_sum(part, tok_rows):
    cols = part.shape[1]
    count = part.shape[0] // tok_rows
    outer = count // 4
    chip = pair_sum(part.reshape(count // 2, 2, tok_rows, cols), 1, count)
    blocks = pair_sum(chip.reshape(outer, 2, tok_rows, cols), 2, count)
    place = lax.axis_index("gx") // 4
    total = lax.dynamic_index_in_dim(blocks, place, 0, keepdims=False).astype(jnp.float32)
    for shift in range(1, outer):
        given = lax.dynamic_index_in_dim(blocks, (place + shift) % outer, 0, keepdims=False)
        peers = [(i, (i // 4 + shift) % outer * 4 + i % 4) for i in range(count)]
        total = total + lax.ppermute(given, "gx", peers).astype(jnp.float32)
    return total


def on_device(
    tokens,
    pre_gain,
    w_q,
    w_k,
    w_v,
    w_o,
    post_gain,
    k_cache,
    v_cache,
    cached_len,
    new_len,
    slot_offset,
):
    tok_rows = tokens.shape[0]
    q_cols, kv_cols = w_q.shape[1], w_k.shape[1]
    n_gy = D // tokens.shape[1]
    gy = lax.axis_index("gy")
    weights = lax.all_gather(jnp.concatenate([w_q, w_k, w_v], axis=1), "gx", axis=0, tiled=True)
    if n_gy == 2:
        swap = [(0, 1), (1, 0)]
        other_in = lax.ppermute(tokens, "gy", swap)
        other_gain = lax.ppermute(pre_gain, "gy", swap)
        whole_in = jnp.where(
            gy == 0,
            jnp.concatenate([tokens, other_in], axis=1),
            jnp.concatenate([other_in, tokens], axis=1),
        )
        whole_gain = jnp.where(
            gy == 0,
            jnp.concatenate([pre_gain, other_gain]),
            jnp.concatenate([other_gain, pre_gain]),
        )
    else:
        whole_in = lax.all_gather(tokens, "gy", axis=1, tiled=True)
        whole_gain = lax.all_gather(pre_gain, "gy", axis=0, tiled=True)
    float_in = whole_in.astype(jnp.float32)
    scale_rows = lax.rsqrt(jnp.mean(float_in * float_in, axis=1, keepdims=True) + epsilon)
    normed = (float_in * scale_rows * (1.0 + whole_gain.astype(jnp.float32))).astype(jnp.bfloat16)
    row_ids = lax.axis_index("gx") * tok_rows + jnp.arange(tok_rows, dtype=jnp.int32)
    request = row_ids // NEWTOK
    within = row_ids % NEWTOK
    owner_mask = request[:, None] == jnp.arange(REQS, dtype=jnp.int32)[None, :]
    row_cached = jnp.sum(jnp.where(owner_mask, cached_len[None, :], 0), axis=1)
    row_fresh = jnp.sum(jnp.where(owner_mask, new_len[None, :], 0), axis=1)
    position = row_cached + within
    half = HD // 2
    inverse = jnp.power(10000.0, -2.0 * jnp.arange(half, dtype=jnp.float32) / HD)
    angle = position.astype(jnp.float32)[:, None] * inverse[None, :]
    cosine, sine = jnp.cos(angle), jnp.sin(angle)
    cosine = jnp.concatenate([cosine, cosine], axis=1)
    sine = jnp.concatenate([-sine, sine], axis=1)
    qkv_new = project(normed, weights, cosine, sine, q_cols, q_cols + kv_cols)
    qkv = lax.all_gather(qkv_new, "gx", axis=0, tiled=True)
    qkv, w_o_t = lax.optimization_barrier((qkv, w_o.T))
    w_out = lax.all_gather(w_o_t, "gx", axis=0, tiled=True)
    slab = k_cache.shape[0]
    first = jnp.full((REQS,), lax.axis_index("gx") * slab, jnp.int32)
    info = jnp.stack([cached_len, new_len, slot_offset, first])
    k_pool, v_pool, num_den = attend(info, qkv, k_cache, v_cache)
    half_cols = (q_cols // HD + 1) // 2 * HD
    sums = jnp.concatenate(
        [
            scatter_sum(num_den[:, :half_cols], tok_rows),
            scatter_sum(num_den[:, half_cols:], tok_rows),
        ],
        axis=1,
    )
    heads = q_cols // HD
    head_num = sums[:, :q_cols].reshape(tok_rows, heads, HD)
    head_den = sums[:, q_cols : q_cols + heads]
    attended = head_num / head_den[:, :, None]
    attended = jnp.where((within < row_fresh)[:, None, None], attended, 0.0)
    attended = attended.reshape(tok_rows, q_cols).astype(jnp.bfloat16)
    if n_gy == 2:
        theirs = lax.ppermute(out_half(attended, w_out, 1 - gy), "gy", swap)
        own = out_half(attended, w_out, gy)
        branch = own.astype(jnp.float32) + theirs.astype(jnp.float32)
        square = jnp.sum(branch * branch, axis=1)
        mean_square = (square + lax.ppermute(square, "gy", swap)) / D
    else:
        partial_out = lax.dot_general(
            attended, w_out, (((1,), (1,)), ((), ())), preferred_element_type=jnp.float32
        ).astype(jnp.bfloat16)
        branch = lax.psum_scatter(partial_out, "gy", scatter_dimension=1, tiled=True).astype(
            jnp.float32
        )
        mean_square = lax.psum(jnp.sum(branch * branch, axis=1), "gy") / D
    layer_out = (
        tokens.astype(jnp.float32)
        + branch * lax.rsqrt(mean_square + epsilon)[:, None] * (1.0 + post_gain.astype(jnp.float32))
    ).astype(jnp.bfloat16)
    return (layer_out, k_pool, v_pool)


def solution(mesh):
    placed = (
        P("gx", "gy"),
        P("gy"),
        P("gx", "gy"),
        P("gx", "gy"),
        P("gx", "gy"),
        P("gy", "gx"),
        P("gy"),
        P("gx", "gy"),
        P("gx", "gy"),
        P(),
        P(),
        P(),
    )
    return jax.shard_map(
        on_device,
        mesh=mesh,
        in_specs=placed,
        out_specs=(P("gx", "gy"), P("gx", "gy"), P("gx", "gy")),
        check_vma=False,
    )
```

```python
import functools

import jax
import jax.numpy as jnp
from jax import lax
from jax.experimental import pallas as pl
from jax.experimental.pallas import tpu as pltpu
from jax.sharding import PartitionSpec as P

D = 4608
HD = 128
REQS = 12
NEWTOK = 192
KB = 256
VMEM_LIMIT = 56 * 1024 * 1024


epsilon = 1e-06
soft_cap = 50.0
query_scale = 144.0 ** (-0.5)


def project_kernel(q_blocks, rope_blocks, x_ref, w_ref, cos_ref, sin_ref, out_ref):
    block = pl.program_id(0)
    lin = jnp.dot(x_ref[...], w_ref[...], preferred_element_type=jnp.float32)
    heads = lin.shape[1] // HD

    @pl.when(block < rope_blocks)
    def _():
        scale = jnp.where(block < q_blocks, query_scale, 1.0)
        cosine = cos_ref[...] * scale
        sine = sin_ref[...] * scale
        for h in range(heads):
            u = lin[:, h * HD : (h + 1) * HD]
            swapped = pltpu.roll(u, HD // 2, 1)
            out_ref[:, h * HD : (h + 1) * HD] = (u * cosine + swapped * sine).astype(
                out_ref.dtype
            )

    @pl.when(block >= rope_blocks)
    def _():
        out_ref[...] = lin.astype(out_ref.dtype)


def project(normed, weights, cosine, sine, q_cols, rope_cols):
    rows, cols = normed.shape[0], weights.shape[1]
    width = min(512, cols - rope_cols)
    return pl.pallas_call(
        functools.partial(project_kernel, q_cols // width, rope_cols // width),
        grid=(cols // width,),
        in_specs=[
            pl.BlockSpec((rows, D), lambda i: (0, 0)),
            pl.BlockSpec((D, width), lambda i: (0, i)),
            pl.BlockSpec((rows, HD), lambda i: (0, 0)),
            pl.BlockSpec((rows, HD), lambda i: (0, 0)),
        ],
        out_specs=pl.BlockSpec((rows, width), lambda i: (0, i)),
        out_shape=jax.ShapeDtypeStruct((rows, cols), jnp.bfloat16),
        compiler_params=pltpu.CompilerParams(vmem_limit_bytes=VMEM_LIMIT),
        cost_estimate=pl.CostEstimate(
            flops=2 * rows * D * cols, bytes_accessed=2 * D * cols, transcendentals=0
        ),
    )(normed, weights, cosine, sine)


def attend_kernel(
    group, slab, info_ref, q_ref, k_ref, v_ref, kc_ref, vc_ref, kp_ref, vp_ref, nd_ref, acc_ref
):
    head = pl.program_id(0)
    gw = group * HD
    rows = group * NEWTOK
    den_at = nd_ref.shape[1] - HD
    kp_ref[...] = kc_ref[...]
    vp_ref[...] = vc_ref[...]
    num_cols = pl.ds(pl.multiple_of(head * gw, HD), gw)
    nd_ref[:, num_cols] = jnp.zeros((nd_ref.shape[0], gw), nd_ref.dtype)

    @pl.when(head == 0)
    def _():
        nd_ref[:, den_at:] = jnp.zeros((nd_ref.shape[0], HD), nd_ref.dtype)

    first = info_ref[3, 0]

    def request(r, carry):
        start = info_ref[2, r] - first
        cached = info_ref[0, r]
        fresh = info_ref[1, r]
        land = start + cached
        stop = land + fresh
        b_first = jnp.maximum(start, 0) // KB
        b_stop = (jnp.clip(stop, 0, slab) + (KB - 1)) // KB
        l_first = jnp.maximum(land, 0) // KB
        row0 = pl.multiple_of(r * NEWTOK, NEWTOK)

        @pl.when(b_stop > b_first)
        def _():
            def write(j, c):
                base = pl.multiple_of(j * KB, KB)
                at = lax.broadcasted_iota(jnp.int32, (KB, NEWTOK), 0) + (base - land)
                col = lax.broadcasted_iota(jnp.int32, (KB, NEWTOK), 1)
                pick = jnp.where((at == col) & (col < fresh), 1.0, 0.0).astype(jnp.bfloat16)
                here = lax.broadcasted_iota(jnp.int32, (KB, HD), 0) + (base - land)
                new = (here >= 0) & (here < fresh)
                for src, dst in ((k_ref, kp_ref), (v_ref, vp_ref)):
                    got = jnp.dot(
                        pick, src[pl.ds(row0, NEWTOK), :], preferred_element_type=jnp.float32
                    )
                    old = dst[pl.ds(base, KB), :].astype(jnp.float32)
                    dst[pl.ds(base, KB), :] = jnp.where(new, got, old).astype(dst.dtype)
                return c

            lax.fori_loop(l_first, b_stop, write, 0)

            acc_ref[...] = jnp.zeros_like(acc_ref)
            q = jnp.concatenate(
                [q_ref[pl.ds(row0, NEWTOK), g * HD : (g + 1) * HD] for g in range(group)], axis=0
            )
            ones = jnp.ones((KB, HD), jnp.bfloat16)
            index = lax.broadcasted_iota(jnp.int32, (rows, KB), 0) % NEWTOK
            last = cached + jnp.minimum(index, fresh - 1)
            slot = lax.broadcasted_iota(jnp.int32, (rows, KB), 1)

            def block(j, c):
                base = pl.multiple_of(j * KB, KB)
                logits = lax.dot_general(
                    q,
                    kp_ref[pl.ds(base, KB), :],
                    (((1,), (1,)), ((), ())),
                    preferred_element_type=jnp.float32,
                )
                weight = jnp.exp(soft_cap * jnp.tanh(logits * (1.0 / soft_cap)))
                at = slot + (base - start)
                weight = jnp.where((at >= 0) & (at <= last), weight, 0.0).astype(jnp.bfloat16)
                values = jnp.concatenate([vp_ref[pl.ds(base, KB), :], ones], axis=1)
                acc_ref[...] += jnp.dot(weight, values, preferred_element_type=jnp.float32)
                return c

            lax.fori_loop(b_first, b_stop, block, 0)
            for g in range(group):
                nd_ref[
                    pl.ds(row0, NEWTOK), pl.ds(pl.multiple_of(head * gw + g * HD, HD), HD)
                ] = acc_ref[g * NEWTOK : (g + 1) * NEWTOK, :HD].astype(nd_ref.dtype)
            lane = lax.broadcasted_iota(jnp.int32, (NEWTOK, HD), 1)
            den = nd_ref[pl.ds(row0, NEWTOK), den_at:].astype(jnp.float32)
            for g in range(group):
                den = jnp.where(
                    lane == head * group + g, acc_ref[g * NEWTOK : (g + 1) * NEWTOK, HD:], den
                )
            nd_ref[pl.ds(row0, NEWTOK), den_at:] = den.astype(nd_ref.dtype)

        return carry

    lax.fori_loop(0, REQS, request, 0)


def attend(info, qkv, k_cache, v_cache):
    slab, kv_cols = k_cache.shape
    total = qkv.shape[0]
    kv = kv_cols // HD
    q_cols = qkv.shape[1] - 2 * kv_cols
    group = q_cols // kv_cols
    pool = pl.BlockSpec((slab, HD), lambda c: (0, c))
    return pl.pallas_call(
        functools.partial(attend_kernel, group, slab),
        grid=(kv,),
        in_specs=[
            pl.BlockSpec(memory_space=pltpu.SMEM),
            pl.BlockSpec((total, group * HD), lambda c: (0, c)),
            pl.BlockSpec((total, HD), lambda c: (0, q_cols // HD + c)),
            pl.BlockSpec((total, HD), lambda c: (0, (q_cols + kv_cols) // HD + c)),
            pool,
            pool,
        ],
        out_specs=[
            pool,
            pool,
            pl.BlockSpec((total, q_cols + HD), lambda c: (0, 0)),
        ],
        out_shape=[
            jax.ShapeDtypeStruct(k_cache.shape, k_cache.dtype),
            jax.ShapeDtypeStruct(v_cache.shape, v_cache.dtype),
            jax.ShapeDtypeStruct((total, q_cols + HD), jnp.bfloat16),
        ],
        scratch_shapes=[pltpu.VMEM((group * NEWTOK, 2 * HD), jnp.float32)],
        compiler_params=pltpu.CompilerParams(vmem_limit_bytes=VMEM_LIMIT),
        cost_estimate=pl.CostEstimate(
            flops=4 * 2 * NEWTOK * slab * q_cols * 2,
            bytes_accessed=2 * total * (2 * q_cols + 2 * kv_cols),
            transcendentals=4 * NEWTOK * slab * q_cols // HD,
        ),
    )(info, qkv, qkv, qkv, k_cache, v_cache)


def out_kernel(half_ref, x_ref, w_ref, out_ref):
    out_ref[...] = lax.dot_general(
        x_ref[...], w_ref[...], (((1,), (1,)), ((), ())), preferred_element_type=jnp.float32
    ).astype(out_ref.dtype)


def out_half(attended, w_out, half):
    rows, depth = attended.shape
    cols = w_out.shape[0] // 2
    width = 384
    steps = cols // width
    return pl.pallas_call(
        out_kernel,
        grid_spec=pltpu.PrefetchScalarGridSpec(
            num_scalar_prefetch=1,
            grid=(steps,),
            in_specs=[
                pl.BlockSpec((rows, depth), lambda i, half: (0, 0)),
                pl.BlockSpec((width, depth), lambda i, half: (half[0] * steps + i, 0)),
            ],
            out_specs=pl.BlockSpec((rows, width), lambda i, half: (0, i)),
        ),
        out_shape=jax.ShapeDtypeStruct((rows, cols), jnp.bfloat16),
        compiler_params=pltpu.CompilerParams(vmem_limit_bytes=VMEM_LIMIT),
        cost_estimate=pl.CostEstimate(
            flops=2 * rows * depth * cols, bytes_accessed=2 * depth * cols, transcendentals=0
        ),
    )(half.reshape(1).astype(jnp.int32), attended, w_out)


def pick_side(blocks, side, start, cols):
    size = (blocks.shape[0], 1, blocks.shape[2], cols)
    return lax.dynamic_slice(blocks, (0, side, 0, start), size)[:, 0]


def pair_sum(blocks, stride, count, start, cols):
    side = lax.axis_index("gx") // stride % 2
    given = pick_side(blocks, 1 - side, start, cols)
    taken = lax.ppermute(given, "gx", [(i, i ^ stride) for i in range(count)])
    kept = pick_side(blocks, side, start, cols)
    return (kept.astype(jnp.float32) + taken.astype(jnp.float32)).astype(jnp.bfloat16)


def scatter_sum(part, tok_rows, start, cols):
    count = part.shape[0] // tok_rows
    outer = count // 4
    chip = pair_sum(part.reshape(count // 2, 2, tok_rows, part.shape[1]), 1, count, start, cols)
    blocks = pair_sum(chip.reshape(outer, 2, tok_rows, cols), 2, count, 0, cols)
    place = lax.axis_index("gx") // 4
    total = lax.dynamic_index_in_dim(blocks, place, 0, keepdims=False).astype(jnp.float32)
    for shift in range(1, outer):
        given = lax.dynamic_index_in_dim(blocks, (place + shift) % outer, 0, keepdims=False)
        peers = [(i, (i // 4 + shift) % outer * 4 + i % 4) for i in range(count)]
        total = total + lax.ppermute(given, "gx", peers).astype(jnp.float32)
    return total


def on_device(
    tokens,
    pre_gain,
    w_q,
    w_k,
    w_v,
    w_o,
    post_gain,
    k_cache,
    v_cache,
    cached_len,
    new_len,
    slot_offset,
):
    tok_rows = tokens.shape[0]
    q_cols, kv_cols = w_q.shape[1], w_k.shape[1]
    n_gy = D // tokens.shape[1]
    gy = lax.axis_index("gy")
    weights = lax.all_gather(jnp.concatenate([w_q, w_k, w_v], axis=1), "gx", axis=0, tiled=True)
    if n_gy == 2:
        swap = [(0, 1), (1, 0)]
        other_in = lax.ppermute(tokens, "gy", swap)
        other_gain = lax.ppermute(pre_gain, "gy", swap)
        whole_in = jnp.where(
            gy == 0,
            jnp.concatenate([tokens, other_in], axis=1),
            jnp.concatenate([other_in, tokens], axis=1),
        )
        whole_gain = jnp.where(
            gy == 0,
            jnp.concatenate([pre_gain, other_gain]),
            jnp.concatenate([other_gain, pre_gain]),
        )
    else:
        whole_in = lax.all_gather(tokens, "gy", axis=1, tiled=True)
        whole_gain = lax.all_gather(pre_gain, "gy", axis=0, tiled=True)
    float_in = whole_in.astype(jnp.float32)
    scale_rows = lax.rsqrt(jnp.mean(float_in * float_in, axis=1, keepdims=True) + epsilon)
    normed = (float_in * scale_rows * (1.0 + whole_gain.astype(jnp.float32))).astype(jnp.bfloat16)
    row_ids = lax.axis_index("gx") * tok_rows + jnp.arange(tok_rows, dtype=jnp.int32)
    request = row_ids // NEWTOK
    within = row_ids % NEWTOK
    owner_mask = request[:, None] == jnp.arange(REQS, dtype=jnp.int32)[None, :]
    row_cached = jnp.sum(jnp.where(owner_mask, cached_len[None, :], 0), axis=1)
    row_fresh = jnp.sum(jnp.where(owner_mask, new_len[None, :], 0), axis=1)
    position = row_cached + within
    half = HD // 2
    inverse = jnp.power(10000.0, -2.0 * jnp.arange(half, dtype=jnp.float32) / HD)
    angle = position.astype(jnp.float32)[:, None] * inverse[None, :]
    cosine, sine = jnp.cos(angle), jnp.sin(angle)
    cosine = jnp.concatenate([cosine, cosine], axis=1)
    sine = jnp.concatenate([-sine, sine], axis=1)
    qkv_new = project(normed, weights, cosine, sine, q_cols, q_cols + kv_cols)
    qkv = lax.all_gather(qkv_new, "gx", axis=0, tiled=True)
    qkv, w_o_t = lax.optimization_barrier((qkv, w_o.T))
    w_out = lax.all_gather(w_o_t, "gx", axis=0, tiled=True)
    slab = k_cache.shape[0]
    first = jnp.full((REQS,), lax.axis_index("gx") * slab, jnp.int32)
    info = jnp.stack([cached_len, new_len, slot_offset, first])
    k_pool, v_pool, num_den = attend(info, qkv, k_cache, v_cache)
    half_cols = (q_cols // HD + 1) // 2 * HD
    sums = jnp.concatenate(
        [
            scatter_sum(num_den, tok_rows, 0, half_cols),
            scatter_sum(num_den, tok_rows, half_cols, q_cols + HD - half_cols),
        ],
        axis=1,
    )
    heads = q_cols // HD
    head_num = sums[:, :q_cols].reshape(tok_rows, heads, HD)
    head_den = sums[:, q_cols : q_cols + heads]
    attended = head_num / head_den[:, :, None]
    attended = jnp.where((within < row_fresh)[:, None, None], attended, 0.0)
    attended = attended.reshape(tok_rows, q_cols).astype(jnp.bfloat16)
    if n_gy == 2:
        theirs = lax.ppermute(out_half(attended, w_out, 1 - gy), "gy", swap)
        own = out_half(attended, w_out, gy)
        branch = own.astype(jnp.float32) + theirs.astype(jnp.float32)
        square = jnp.sum(branch * branch, axis=1)
        mean_square = (square + lax.ppermute(square, "gy", swap)) / D
    else:
        partial_out = lax.dot_general(
            attended, w_out, (((1,), (1,)), ((), ())), preferred_element_type=jnp.float32
        ).astype(jnp.bfloat16)
        branch = lax.psum_scatter(partial_out, "gy", scatter_dimension=1, tiled=True).astype(
            jnp.float32
        )
        mean_square = lax.psum(jnp.sum(branch * branch, axis=1), "gy") / D
    layer_out = (
        tokens.astype(jnp.float32)
        + branch * lax.rsqrt(mean_square + epsilon)[:, None] * (1.0 + post_gain.astype(jnp.float32))
    ).astype(jnp.bfloat16)
    return (layer_out, k_pool, v_pool)


def solution(mesh):
    placed = (
        P("gx", "gy"),
        P("gy"),
        P("gx", "gy"),
        P("gx", "gy"),
        P("gx", "gy"),
        P("gy", "gx"),
        P("gy"),
        P("gx", "gy"),
        P("gx", "gy"),
        P(),
        P(),
        P(),
    )
    return jax.shard_map(
        on_device,
        mesh=mesh,
        in_specs=placed,
        out_specs=(P("gx", "gy"), P("gx", "gy"), P("gx", "gy")),
        check_vma=False,
    )
```
